256 devices in a mesh: member: 16 (over x, z_lo), tensor: 16 (over y, z_hi, core).
Axes of the slice: x: 4, y: 4, z: 8 (z_hi: 2, z_lo: 4; z = z_hi * 4 + z_lo), core: 2. Of those that a mesh axis runs over, the one named last changes fastest.
Arguments:
- tokens: bfloat16 [2048, 8192], P('member'), may hold values from -6 to 6
- out_grad: bfloat16 [2048, 8192], P('member'), may hold values from -6 to 6
- flip_bits: int32 [2048], P('member'), may hold values 0 or 1
- in_scale: float32 [16, 8192], P(None, 'member'), may hold values from 0.5 to 2
- out_scale: float32 [16, 8192], P(None, 'member'), may hold values from 0.5 to 2
- gate_scale: float32 [16, 14336], P('member', 'tensor'), may hold values from 0.5 to 2
- gate_flip: float32 [16, 14336], P('member', 'tensor'), may hold values from -2 to 2
- up_scale: float32 [16, 14336], P('member', 'tensor'), may hold values from 0.5 to 2
- up_flip: float32 [16, 14336], P('member', 'tensor'), may hold values from -2 to 2
- proj_gate: bfloat16 [2048, 14336], P('member', 'tensor'), may hold values from -6 to 6
- proj_up: bfloat16 [2048, 14336], P('member', 'tensor'), may hold values from -6 to 6
- w_gate: bfloat16 [8192, 14336], P('member', 'tensor'), may hold values from -0.0625 to 0.0625
- w_up: bfloat16 [8192, 14336], P('member', 'tensor'), may hold values from -0.0625 to 0.0625
- w_down: bfloat16 [14336, 8192], P('tensor', 'member'), may hold values from -0.046875 to 0.046875
Outputs:
- x_grad: bfloat16 [2048, 8192], P(('member', 'tensor'))
- w_gate_grad: bfloat16 [8192, 14336], P('member', 'tensor')
- w_up_grad: bfloat16 [8192, 14336], P('member', 'tensor')
- w_down_grad: bfloat16 [14336, 8192], P('tensor', 'member')
- in_scale_grad: float32 [16, 8192], P(None, 'member')
- out_scale_grad: float32 [16, 8192], P(None, 'member')
- gate_scale_grad: float32 [16, 14336], P('member', 'tensor')
- gate_flip_grad: float32 [16, 14336], P('member', 'tensor')
- up_scale_grad: float32 [16, 14336], P('member', 'tensor')
- up_flip_grad: float32 [16, 14336], P('member', 'tensor')
The draws below stay inside these ranges and needn't reach their ends.
All inputs are finite; a program needn't handle non-finite values. No bound on the sum of `flip_bits` on one device may be relied on, other than what follows from the above.
Results may differ from the reference program's by a relative error of at most 0.024.
Values may be sent and summed in bfloat16 or wider, within the bound.
No kernel may reach another device: no remote copies, remote signals or barrier semaphores. Data moves between devices by JAX's collectives and lax.ppermute only.
A program may use at most 128 MiB of HBM per device.

```python
import math
import jax
import jax.numpy as jnp

D = 8192
FF = 14336
TOK = 128
MEMBERS = 16
TOKENS = 2048


def touch_ends(result, key, low, high):
    place = [jax.random.randint(jax.random.fold_in(key, axis), (), 0, length) for axis, length in enumerate(result.shape)]
    main_axis = result.shape.index(max(result.shape))
    neighbour = place[:main_axis] + [(place[main_axis] + 1) % result.shape[main_axis]] + place[main_axis + 1:]
    return result.at[tuple(place)].set(low).at[tuple(neighbour)].set(high)


def shard_levels(own_key, shape, cuts, smallest, largest):
    level, own = 1.0, jax.random.fold_in(own_key, 6)
    for position, parts in cuts:
        draws = jnp.exp(jax.random.uniform(jax.random.fold_in(own, position), (parts,), jnp.float32, smallest / len(cuts), largest / len(cuts)))
        level = level * jnp.repeat(draws, shape[position] // parts).reshape([-1 if axis == position else 1 for axis in range(len(shape))])
    return level


def centred(key, extent, width, reach, pieces=(), kind=jnp.bfloat16):
    array = jax.random.normal(key, extent, jnp.float32) * width
    if len(pieces) > 0:
        array = shard_levels(key, extent, pieces, -0.22, 0.18) * array
    return jnp.clip(array, min=-reach, max=reach).astype(kind)


def setup_inputs(seed: int = 0) -> dict:
    splits = jax.random.split(jax.random.key(seed), 15)
    tokens = centred(splits[0], (TOKENS, D), 1.0, 6.0, ((0, 16),))
    out_grad = centred(splits[1], (TOKENS, D), 1.0, 6.0, ((0, 16),))
    flip_bits = touch_ends((jax.random.randint(splits[2], (TOKENS,), 0, 2) < 1).astype(jnp.int32), jax.random.fold_in(splits[2], 1), 0, 1)
    in_scale = jnp.clip(jnp.exp(math.log(2.0) - 1.3862944 * jax.random.uniform(splits[3], (MEMBERS, D), jnp.float32) ** shard_levels(splits[3], (MEMBERS, D), ((1, 16),), -0.2, 0.2)), 0.5, 2.0)
    out_scale = jnp.clip(jnp.exp(math.log(2.0) - 1.3862944 * jax.random.uniform(splits[4], (MEMBERS, D), jnp.float32) ** shard_levels(splits[4], (MEMBERS, D), ((1, 16),), -0.2, 0.2)), 0.5, 2.0)
    gate_scale = jnp.clip(jnp.exp(math.log(2.0) - 1.3862944 * jax.random.uniform(splits[5], (MEMBERS, FF), jnp.float32) ** shard_levels(splits[5], (MEMBERS, FF), ((0, 16), (1, 16)), -0.2, 0.2)), 0.5, 2.0)
    gate_flip = centred(splits[6], (MEMBERS, FF), 0.5, 2.0, ((0, 16), (1, 16)), jnp.float32)
    up_scale = jnp.clip(jnp.exp(math.log(2.0) - 1.3862944 * jax.random.uniform(splits[7], (MEMBERS, FF), jnp.float32) ** shard_levels(splits[7], (MEMBERS, FF), ((0, 16), (1, 16)), -0.2, 0.2)), 0.5, 2.0)
    up_flip = centred(splits[8], (MEMBERS, FF), 0.5, 2.0, ((0, 16), (1, 16)), jnp.float32)
    proj_gate = centred(splits[9], (TOKENS, FF), 1.0, 6.0, ((0, 16), (1, 16)))
    proj_up = centred(splits[10], (TOKENS, FF), 1.0, 6.0, ((0, 16), (1, 16)))
    w_gate = centred(splits[11], (D, FF), D ** -0.5, 0.0625, ((0, 16), (1, 16)))
    w_up = centred(splits[12], (D, FF), D ** -0.5, 0.0625, ((0, 16), (1, 16)))
    w_down = centred(splits[13], (FF, D), FF ** -0.5, 0.046875, ((0, 16), (1, 16)))
    return dict(tokens=tokens, out_grad=out_grad, flip_bits=flip_bits, in_scale=in_scale, out_scale=out_scale, gate_scale=gate_scale, gate_flip=gate_flip, up_scale=up_scale, up_flip=up_flip, proj_gate=proj_gate, proj_up=proj_up, w_gate=w_gate, w_up=w_up, w_down=w_down)


def per_member(values):
    return values.reshape(MEMBERS, TOK, values.shape[-1]).sum(axis=1)


def reference(tokens, out_grad, flip_bits, in_scale, out_scale, gate_scale, gate_flip, up_scale, up_flip, proj_gate, proj_up, w_gate, w_up, w_down):
    def spread(table):
        return jnp.repeat(table, TOK, axis=0)

    sign = (2 * flip_bits - 1).astype(jnp.float32)[:, None]
    gate_factor = spread(gate_scale) + sign * spread(gate_flip)
    up_factor = spread(up_scale) + sign * spread(up_flip)
    pg_f = proj_gate.astype(jnp.float32)
    pu_f = proj_up.astype(jnp.float32)
    gate = pg_f * gate_factor
    up = pu_f * up_factor
    sig = jax.nn.sigmoid(gate)
    act = gate * sig
    hidden = (act * up).astype(jnp.bfloat16)
    in_rows = (tokens.astype(jnp.float32) * spread(in_scale)).astype(jnp.bfloat16)
    grad_z = (out_grad.astype(jnp.float32) * spread(out_scale)).astype(jnp.bfloat16)
    grad_hidden = jnp.dot(grad_z, w_down.T, preferred_element_type=jnp.float32)
    grad_gate = grad_hidden * up * sig * (1.0 + gate * (1.0 - sig))
    grad_up = grad_hidden * act
    gate_scale_grad = per_member(grad_gate * pg_f)
    gate_flip_grad = per_member(sign * grad_gate * pg_f)
    up_scale_grad = per_member(grad_up * pu_f)
    up_flip_grad = per_member(sign * grad_up * pu_f)
    grad_pg = (grad_gate * gate_factor).astype(jnp.bfloat16)
    grad_pu = (grad_up * up_factor).astype(jnp.bfloat16)
    w_gate_grad = jnp.dot(in_rows.T, grad_pg, preferred_element_type=jnp.float32).astype(jnp.bfloat16)
    w_up_grad = jnp.dot(in_rows.T, grad_pu, preferred_element_type=jnp.float32).astype(jnp.bfloat16)
    w_down_grad = jnp.dot(hidden.T, grad_z, preferred_element_type=jnp.float32).astype(jnp.bfloat16)
    grad_in = jnp.dot(grad_pg, w_gate.T, preferred_element_type=jnp.float32) + jnp.dot(grad_pu, w_up.T, preferred_element_type=jnp.float32)
    x_grad = (grad_in * spread(in_scale)).astype(jnp.bfloat16)
    in_scale_grad = per_member(tokens.astype(jnp.float32) * grad_in)
    down_out = jnp.dot(hidden, w_down, preferred_element_type=jnp.float32)
    out_scale_grad = per_member(out_grad.astype(jnp.float32) * down_out)
    return (x_grad, w_gate_grad, w_up_grad, w_down_grad, in_scale_grad, out_scale_grad, gate_scale_grad, gate_flip_grad, up_scale_grad, up_flip_grad)
```

```python
import functools

import jax
import jax.numpy as jnp
from jax import lax
from jax.sharding import Mesh, PartitionSpec as P

AXES = ("mx", "mz", "ty", "th", "tc")
SIZES = {"mx": 4, "mz": 4, "ty": 4, "th": 2, "tc": 2}
CHUNKS = ((0, 1), (2, 3))


def shift(value, axis, step):
    size = SIZES[axis]
    return lax.ppermute(value, axis, [(i, (i + step) % size) for i in range(size)])


def back_order(value, dim, index):
    size = value.shape[dim]
    flipped = jnp.flip(value, dim)
    return lax.dynamic_slice_in_dim(jnp.concatenate([flipped, flipped], dim), size - 1 - index, size, dim)


def forth_order(value, dim, index):
    size = value.shape[dim]
    return lax.dynamic_slice_in_dim(
        jnp.concatenate([value, value], dim), lax.rem(size - index, size), size, dim
    )


def contract_rows(left, right):
    return lax.dot_general(left, right, (((0,), (0,)), ((), ())), preferred_element_type=jnp.float32)


def contract_cols(left, right):
    return lax.dot_general(left, right, (((1,), (1,)), ((), ())), preferred_element_type=jnp.float32)


def to_members(rows, x, z):
    wide = rows.shape[1] // 4
    width = wide // 4
    parts = [
        lax.dynamic_slice_in_dim(rows, lax.rem(x + k, 4) * wide, wide, 1) for k in range(4)
    ]
    got = jnp.stack([parts[0]] + [shift(parts[k], "mx", k) for k in (1, 2, 3)])
    parts = [
        lax.dynamic_slice_in_dim(got, lax.rem(z + k, 4) * width, width, 2) for k in range(4)
    ]
    return jnp.stack([parts[0]] + [shift(parts[k], "mz", k) for k in (1, 2, 3)], axis=1)


def from_members(block, x, z):
    rows, width = block.shape[2:]
    got = jnp.stack([block[0]] + [shift(block[k], "mx", -k) for k in (1, 2, 3)])
    got = jnp.stack([got[:, 0]] + [shift(got[:, k], "mz", -k) for k in (1, 2, 3)], axis=1)
    got = forth_order(forth_order(got, 0, x), 1, z)
    return jnp.transpose(got, (2, 0, 1, 3)).reshape(rows, 16 * width)


def add(*terms):
    total = terms[0].astype(jnp.float32)
    for term in terms[1:]:
        total = total + term.astype(jnp.float32)
    return total


def flat(*blocks):
    return jnp.concatenate([block.reshape(-1, block.shape[-1]) for block in blocks])


def exchange(axis, step, *blocks):
    got = shift(flat(*blocks), axis, step)
    out, start = [], 0
    for block in blocks:
        rows = block.size // block.shape[-1]
        out.append(got[start : start + rows].reshape(block.shape))
        start += rows
    return out


def sum_tensor(value):
    value = value + shift(value, "tc", 1)
    value = value + shift(value, "th", 1)
    value = value + shift(value, "ty", 2)
    return value + shift(value, "ty", 1)


def local(
    tokens,
    out_grad,
    flip_bits,
    in_scale,
    out_scale,
    gate_scale,
    gate_flip,
    up_scale,
    up_flip,
    proj_gate,
    proj_up,
    w_gate,
    w_up,
    w_down,
):
    x, z, y, h, c = (lax.axis_index(axis) for axis in AXES)
    tok = tokens.shape[0]
    members, width = in_scale.shape
    units = proj_gate.shape[1]
    sub = tok // 16
    f32, bf16 = jnp.float32, jnp.bfloat16

    def relative_rows(value):
        value = value.reshape(4, 2, 2, sub, -1)
        value = back_order(back_order(back_order(value, 0, y), 1, h), 2, c)
        return jnp.transpose(value, (0, 2, 1, 3, 4)).reshape(tok, -1)

    def relative_table(table):
        table = back_order(back_order(table.reshape(4, 4, width), 0, x), 1, z)
        return table.reshape(members, width)

    def own_rows(value):
        first = lax.dynamic_slice_in_dim(value, (4 * y + 2 * h + c) * sub, sub, 0)
        second = lax.dynamic_slice_in_dim(value, (4 * y + 2 * (1 - h) + c) * sub, sub, 0)
        return jnp.concatenate([first, second])

    in_rel, out_rel = relative_table(in_scale), relative_table(out_scale)

    both_own = to_members(jnp.concatenate([own_rows(out_grad), own_rows(tokens)]), x, z)
    both_own = both_own.reshape(members, 4 * sub, width)

    def over_tensor(own):
        blocks = [own] + [shift(own, "ty", j) for j in (1, 2, 3)]
        out = []
        for chunk in CHUNKS:
            mine = jnp.stack([blocks[j] for j in chunk], axis=1)
            out.append(jnp.stack([mine, shift(mine, "tc", 1)], axis=2))
        return out

    cot = over_tensor(both_own[:, : 2 * sub])
    grad_z = [(part.astype(f32) * out_rel[:, None, None, None, :]).astype(bf16) for part in cot]
    half = tok // 2
    partial = [
        contract_cols(part.reshape(members * half, width), w_down).astype(bf16).reshape(4, 4, half, units)
        for part in grad_z
    ]

    sign = (2 * flip_bits - 1).astype(f32)[:, None]
    sign = relative_rows(sign)
    pg_own, pu_own = relative_rows(proj_gate), relative_rows(proj_up)
    tables = jnp.concatenate([gate_scale, gate_flip, up_scale, up_flip])
    high = lax.reduce_precision(tables, 8, 7)
    gate_piece = jnp.concatenate(
        [
            pg_own,
            high.astype(bf16),
            (tables - high).astype(bf16),
            jnp.pad(sign.reshape(1, tok), ((0, 7), (0, units - tok))).astype(bf16),
        ]
    )
    long = tok + 16
    pair = jnp.concatenate([gate_piece, pu_own])
    middle = pair.shape[0] // 2
    gate_z = [shift(gate_piece, "mz", k) for k in (1, 2, 3)]
    pair_r, pair_l = shift(pair, "mx", 1), shift(pair, "mx", -1)
    up_z = [shift(pu_own, "mz", k) for k in (1, 2, 3)]

    first, second = partial
    near_b, plain_b, pair_fr, gate_r1 = exchange("mx", 1, first[2, 2:], first[3, :2], pair_r[:middle], gate_z[0])
    near_a, plain_a, pair_fl, gate_l1 = exchange("mx", -1, first[2, :2], first[1, 2:], pair_l[middle:], gate_z[0])
    sum_b = add(first[3, 2:], near_b).astype(bf16)
    sum_a = add(first[1, :2], near_a).astype(bf16)
    sum_b, next_b, next_pb, gate_r2, gate_r3 = exchange("mx", 1, sum_b, second[2, 2:], second[3, :2], gate_z[1], gate_z[2])
    sum_a, next_a, next_pa, gate_l2, gate_l3 = exchange("mx", -1, sum_a, second[2, :2], second[1, 2:], gate_z[1], gate_z[2])
    line_a = jnp.concatenate([add(first[0, :2], sum_a, plain_b), add(first[0, 2:], plain_a, sum_b)])
    sum_b = add(second[3, 2:], next_b).astype(bf16)
    sum_a = add(second[1, :2], next_a).astype(bf16)
    gate_r, gate_l = flat(gate_r1, gate_r2, gate_r3), flat(gate_l1, gate_l2, gate_l3)
    cut = gate_r.shape[0] // 2
    sum_b, gate_fr = exchange("mx", 1, sum_b, gate_r[:cut])
    sum_a, gate_fl = exchange("mx", -1, sum_a, gate_l[cut:])
    line_b = jnp.concatenate([add(second[0, :2], sum_a, next_pb), add(second[0, 2:], next_pa, sum_b)])
    sent = line_a.astype(bf16)
    own_a = add(line_a[0], *[shift(sent[k], "mz", -k) for k in (1, 2, 3)])
    wide_a = own_a.astype(bf16)
    up_rest = flat(*up_z)
    up_r, up_l = shift(up_rest, "mx", 1), shift(up_rest, "mx", -1)
    sent = line_b.astype(bf16)
    got = [exchange("mz", k, sent[4 - k], wide_a) for k in (1, 2, 3)]
    own_b = add(line_b[0], *[part[0] for part in got])
    wide_b = own_b.astype(bf16)
    spread_a = jnp.stack([wide_a] + [part[1] for part in got])
    cut = up_rest.shape[0] // 2
    a_r, up_fr = exchange("mx", 1, spread_a, up_r[:cut])
    a_l, up_fl = exchange("mx", -1, spread_a, up_l[cut:])
    spread_b = jnp.stack([wide_b] + [shift(wide_b, "mz", k) for k in (1, 2, 3)])
    a_fr, b_r = exchange("mx", 1, a_r[:2], spread_b)
    a_fl, b_l = exchange("mx", -1, a_l[2:], spread_b)
    b_fr, b_fl = shift(b_r[:2], "mx", 1), shift(b_l[2:], "mx", -1)
    spread = [
        flat(spread_a, a_r, a_fr, a_fl, a_l).reshape(members, half, units),
        flat(spread_b, b_r, b_fr, b_fl, b_l).reshape(members, half, units),
    ]
    grad_hidden = jnp.concatenate([own_a, own_b])

    pair_f = jnp.concatenate([pair_fr, pair_fl])
    gate_all = flat(
        gate_piece, *gate_z, pair_r[:long], gate_r, pair_f[:long], gate_fr, gate_fl, pair_l[:long], gate_l
    ).reshape(members, long, units)
    up_all = flat(
        pu_own, up_rest, pair_r[long:], up_r, pair_f[long:], up_fr, up_fl, pair_l[long:], up_l
    ).reshape(members, tok, units)

    table = gate_all[:, tok : tok + 4].astype(f32) + gate_all[:, tok + 4 : tok + 8].astype(f32)
    signs = gate_all[:, tok + 8, :tok].astype(f32)[:, :, None]
    hidden, gate_term, up_term = [], [], []
    for rows in (slice(0, half), slice(half, tok)):
        gate_factor = table[:, 0:1] + signs[:, rows] * table[:, 1:2]
        up_factor = table[:, 2:3] + signs[:, rows] * table[:, 3:4]
        gate = gate_all[:, rows].astype(f32) * gate_factor
        up = up_all[:, rows].astype(f32) * up_factor
        sig = jax.nn.sigmoid(gate)
        act = gate * sig
        hidden.append((act * up).astype(bf16).reshape(-1, units))
        gate_term.append((up * sig * (1.0 + gate * (1.0 - sig)) * gate_factor).astype(bf16))
        up_term.append((act * up_factor).astype(bf16))

    tok_all = over_tensor(both_own[:, 2 * sub :])
    in_rows = [(part.astype(f32) * in_rel[:, None, None, None, :]).astype(bf16) for part in tok_all]

    down_acc, out_terms = 0.0, 0.0
    for hid, part, scaled in zip(hidden, cot, grad_z):
        down_acc = down_acc + contract_rows(hid, scaled.reshape(-1, width))
        down = jnp.dot(hid, w_down, preferred_element_type=f32).reshape(members, half, width)
        out_terms = out_terms + (part.reshape(members, half, width).astype(f32) * down).sum(axis=1)

    gate_acc, up_acc, in_terms, back = 0.0, 0.0, 0.0, [None] * 4
    for number, chunk in enumerate(CHUNKS):
        wide = spread[number].astype(f32)
        pg = (wide * gate_term[number].astype(f32)).astype(bf16).reshape(-1, units)
        pu = (wide * up_term[number].astype(f32)).astype(bf16).reshape(-1, units)
        grad_in = contract_cols(pg, w_gate) + contract_cols(pu, w_up)
        scaled = in_rows[number].reshape(-1, width)
        gate_acc = gate_acc + contract_rows(scaled, pg)
        up_acc = up_acc + contract_rows(scaled, pu)
        grad_in = grad_in.reshape(members, len(chunk), 2, 2 * sub, width)
        in_terms = in_terms + (tok_all[number].astype(f32) * grad_in).sum(axis=(1, 2, 3))
        core = add(grad_in[:, :, 0], shift(grad_in[:, :, 1].astype(bf16), "tc", 1))
        for place, j in enumerate(chunk):
            block = core[:, place]
            back[j] = block if j == 0 else shift(block.astype(bf16), "ty", -j)
    in_sum, out_sum = sum_tensor(jnp.stack([in_terms, out_terms]))

    total = add(*back)
    inner = add(total[:, :sub], shift(total[:, sub:].astype(bf16), "th", 1))
    inner = (inner * in_rel[:, None, :]).astype(bf16)
    x_grad = from_members(inner.reshape(4, 4, sub, width), x, z)

    def absolute_table(table):
        table = table.reshape(4, 4, width)
        return back_order(back_order(table, 0, x), 1, z).reshape(members, width)

    pg_f, pu_f = pg_own.astype(f32), pu_own.astype(f32)
    gate = pg_f * (gate_scale + sign * gate_flip)
    up = pu_f * (up_scale + sign * up_flip)
    sig = jax.nn.sigmoid(gate)
    gate_rows = grad_hidden * up * sig * (1.0 + gate * (1.0 - sig)) * pg_f
    up_rows = grad_hidden * gate * sig * pu_f
    return (
        x_grad,
        gate_acc.astype(bf16),
        up_acc.astype(bf16),
        down_acc.astype(bf16),
        absolute_table(in_sum),
        absolute_table(out_sum),
        jnp.sum(gate_rows, axis=0, keepdims=True),
        jnp.sum(sign * gate_rows, axis=0, keepdims=True),
        jnp.sum(up_rows, axis=0, keepdims=True),
        jnp.sum(sign * up_rows, axis=0, keepdims=True),
    )


def solution(mesh):
    fine = Mesh(mesh.devices.reshape(tuple(SIZES[axis] for axis in AXES)), AXES)
    member, tensor = ("mx", "mz"), ("ty", "th", "tc")
    both = P(member, tensor)
    return jax.shard_map(
        local,
        mesh=fine,
        in_specs=(
            P(member, None),
            P(member, None),
            P(member),
            P(None, member),
            P(None, member),
            both,
            both,
            both,
            both,
            both,
            both,
            both,
            both,
            P(tensor, member),
        ),
        out_specs=(
            P(member + tensor, None),
            both,
            both,
            P(tensor, member),
            P(None, member),
            P(None, member),
            both,
            both,
            both,
            both,
        ),
        check_vma=False,
    )
```

```python
import functools

import jax
import jax.numpy as jnp
from jax import lax
from jax.sharding import Mesh, PartitionSpec as P

AXES = ("mx", "mz", "ty", "th", "tc")
SIZES = {"mx": 4, "mz": 4, "ty": 4, "th": 2, "tc": 2}
CHUNKS = ((0, 1), (2, 3))


def shift(value, axis, step):
    size = SIZES[axis]
    return lax.ppermute(value, axis, [(i, (i + step) % size) for i in range(size)])


def back_order(value, dim, index):
    size = value.shape[dim]
    flipped = jnp.flip(value, dim)
    return lax.dynamic_slice_in_dim(jnp.concatenate([flipped, flipped], dim), size - 1 - index, size, dim)


def contract_rows(left, right):
    return lax.dot_general(left, right, (((0,), (0,)), ((), ())), preferred_element_type=jnp.float32)


def contract_cols(left, right):
    return lax.dot_general(left, right, (((1,), (1,)), ((), ())), preferred_element_type=jnp.float32)


def to_columns(rows, x):
    wide = rows.shape[1] // 4
    parts = [lax.dynamic_slice_in_dim(rows, lax.rem(x + k, 4) * wide, wide, 1) for k in range(4)]
    return jnp.stack([parts[0]] + [shift(parts[k], "mx", k) for k in (1, 2, 3)])


def to_members(got, z):
    width = got.shape[2] // 4
    parts = [lax.dynamic_slice_in_dim(got, lax.rem(z + k, 4) * width, width, 2) for k in range(4)]
    return jnp.stack([parts[0]] + [shift(parts[k], "mz", k) for k in (1, 2, 3)], axis=1)


def hold(value, *others):
    return lax.optimization_barrier((value, *others))[0]


def add(*terms):
    total = terms[0].astype(jnp.float32)
    for term in terms[1:]:
        total = total + term.astype(jnp.float32)
    return total


def flat(*blocks):
    return jnp.concatenate([block.reshape(-1, block.shape[-1]) for block in blocks])


def split(got, blocks):
    out, start = [], 0
    for block in blocks:
        rows = block.size // block.shape[-1]
        out.append(got[start : start + rows].reshape(block.shape))
        start += rows
    return out


def exchange(axis, step, *blocks):
    return split(shift(flat(*blocks), axis, step), blocks)


def both_ways(right, left):
    sent = lax.optimization_barrier((flat(*right), flat(*left)))
    got = lax.optimization_barrier((shift(sent[0], "mx", 1), shift(sent[1], "mx", -1)))
    return split(got[0], right) + split(got[1], left)


def along_z(*values):
    return lax.optimization_barrier(tuple(shift(value, "mz", k + 1) for k, value in enumerate(values)))


def local(
    tokens,
    out_grad,
    flip_bits,
    in_scale,
    out_scale,
    gate_scale,
    gate_flip,
    up_scale,
    up_flip,
    proj_gate,
    proj_up,
    w_gate,
    w_up,
    w_down,
):
    x, z, y, h, c = (lax.axis_index(axis) for axis in AXES)
    tok = tokens.shape[0]
    members, width = in_scale.shape
    units = proj_gate.shape[1]
    sub = tok // 16
    f32, bf16 = jnp.float32, jnp.bfloat16

    def relative_rows(value):
        value = value.reshape(4, 2, 2, sub, -1)
        value = back_order(back_order(back_order(value, 0, y), 1, h), 2, c)
        return jnp.transpose(value, (0, 2, 1, 3, 4)).reshape(tok, -1)

    def relative_table(table):
        table = back_order(back_order(table.reshape(4, 4, width), 0, x), 1, z)
        return table.reshape(members, width)

    def own_rows(value, *steps):
        parts = []
        for step in steps:
            place = lax.rem(y + 4 - step, 4)
            for part in (h, 1 - h):
                parts.append(lax.dynamic_slice_in_dim(value, (4 * place + 2 * part + c) * sub, sub, 0))
        return jnp.concatenate(parts)

    in_rel, out_rel = relative_table(in_scale), relative_table(out_scale)

    sign = (2 * flip_bits - 1).astype(f32)[:, None]
    sign = relative_rows(sign)
    pg_own, pu_own = relative_rows(proj_gate), relative_rows(proj_up)
    tables = jnp.concatenate([gate_scale, gate_flip, up_scale, up_flip])
    high = lax.reduce_precision(tables, 8, 7)
    gate_piece = jnp.concatenate(
        [
            pg_own,
            high.astype(bf16),
            (tables - high).astype(bf16),
            jnp.pad(sign.reshape(1, tok), ((0, 7), (0, units - tok))).astype(bf16),
        ]
    )
    long = tok + 16
    half = tok // 2
    pair = jnp.concatenate([gate_piece, pu_own])
    middle = pair.shape[0] // 2

    def cores(mine):
        return jnp.stack([mine, shift(mine, "tc", 1)], axis=2)

    both_x = to_columns(jnp.concatenate([own_rows(out_grad, 0, 1), own_rows(tokens, 0)]), x)
    cot_x, tok_x = both_x[:, : 4 * sub], both_x[:, 4 * sub :]
    gate_1 = shift(gate_piece, "mz", 1)
    cot_x, pair, pu_own, gate_1 = lax.optimization_barrier((cot_x, pair, pu_own, gate_1))
    pair_r, pair_l = shift(pair, "mx", 1), shift(pair, "mx", -1)
    cot_own = to_members(cot_x, z).reshape(members, 2, 2 * sub, width)
    cot_own, pair_r, pair_l, gate_piece = lax.optimization_barrier((cot_own, pair_r, pair_l, gate_piece))
    gate_z = [gate_1] + [shift(gate_piece, "mz", k) for k in (2, 3)]
    pair_fr, pair_fl = shift(pair_r[:middle], "mx", 1), shift(pair_l[middle:], "mx", -1)
    cot_far = shift(cot_own, "ty", 2)
    tok_own = to_members(hold(tok_x, cot_own), z).reshape(members, 2 * sub, width)

    def partial_sums(part):
        rows = (part.astype(f32) * out_rel[:, None, None, None, :]).astype(bf16).reshape(members * half, width)
        return rows, contract_cols(rows, w_down).astype(bf16).reshape(4, 4, half, units)

    cot_a = cores(cot_own)
    scaled_a, first = partial_sums(cot_a)
    first, pair_fr, pair_fl = lax.optimization_barrier((first, pair_fr, pair_fl))
    near_b, plain_b, gate_r1, near_a, plain_a, gate_l1 = both_ways(
        [first[2, 2:], first[3, :2], gate_1], [first[2, :2], first[1, 2:], gate_1]
    )
    cot_b = cores(cot_far)
    scaled_b, second = partial_sums(cot_b)
    tok_y = lax.all_gather(tok_own, ("ty", "tc")).reshape(4, 2, members, 2 * sub, width)
    near_a, near_b, pu_own = lax.optimization_barrier((near_a, near_b, pu_own))
    up_z = along_z(pu_own, pu_own, pu_own)
    sum_b = add(first[3, 2:], near_b).astype(bf16)
    sum_a = add(first[1, :2], near_a).astype(bf16)
    sum_b, next_b, next_pb, gate_r2, gate_r3, sum_a, next_a, next_pa, gate_l2, gate_l3 = both_ways(
        [sum_b, second[2, 2:], second[3, :2], gate_z[1], gate_z[2]],
        [sum_a, second[2, :2], second[1, 2:], gate_z[1], gate_z[2]],
    )
    line_a = jnp.concatenate([add(first[0, :2], sum_a, plain_b), add(first[0, 2:], plain_a, sum_b)])
    up_z = lax.optimization_barrier((sum_a, sum_b, *up_z))[2:]
    sum_b = add(second[3, 2:], next_b).astype(bf16)
    sum_a = add(second[1, :2], next_a).astype(bf16)
    gate_r, gate_l = flat(gate_r1, gate_r2, gate_r3), flat(gate_l1, gate_l2, gate_l3)
    cut = gate_r.shape[0] // 2
    sum_b, gate_fr, sum_a, gate_fl = both_ways([sum_b, gate_r[:cut]], [sum_a, gate_l[cut:]])
    line_b = jnp.concatenate([add(second[0, :2], sum_a, next_pb), add(second[0, 2:], next_pa, sum_b)])
    sent = line_a.astype(bf16)
    own_a = add(line_a[0], *along_z(sent[3], sent[2], sent[1]))
    wide_a = own_a.astype(bf16)
    up_rest = flat(*up_z)
    up_r, up_l = both_ways([up_rest], [up_rest])
    sent = line_b.astype(bf16)
    got = along_z(*[flat(sent[4 - k], wide_a) for k in (1, 2, 3)])
    got = [split(part, [wide_a, wide_a]) for part in got]
    own_b = add(line_b[0], *[part[0] for part in got])
    wide_b = own_b.astype(bf16)
    spread_a = jnp.stack([wide_a] + [part[1] for part in got])
    tok_y = [
        [
            lax.dynamic_slice(tok_y, (lax.rem(y + 4 - j, 4), lax.rem(c + k, 2), 0, 0, 0), (1, 1) + tok_own.shape)[0, 0]
            for k in range(2)
        ]
        for j in range(4)
    ]
    tok_all = [
        jnp.stack([jnp.stack(tok_y[j], axis=1) for j in chunk], axis=1) for chunk in CHUNKS
    ]
    in_rows = [
        (part.astype(f32) * in_rel[:, None, None, None, :]).astype(bf16).reshape(-1, width) for part in tok_all
    ]
    cut = up_rest.shape[0] // 2
    a_r, up_fr, a_l, up_fl = both_ways([spread_a, up_r[:cut]], [spread_a, up_l[cut:]])
    spread_b = jnp.stack([wide_b, *along_z(wide_b, wide_b, wide_b)])
    a_fr, b_r, a_fl, b_l = both_ways([a_r[:2], spread_b], [a_l[2:], spread_b])
    b_fr, b_fl = both_ways([b_r[:2]], [b_l[2:]])

    pair_f = jnp.concatenate([pair_fr, pair_fl])
    gates = [
        flat(gate_piece, *gate_z),
        flat(pair_r[:long], gate_r),
        flat(pair_f[:long], gate_fr, gate_fl),
        flat(pair_l[:long], gate_l),
    ]
    ups = [
        flat(pu_own, up_rest),
        flat(pair_r[long:], up_r),
        flat(pair_f[long:], up_fr, up_fl),
        flat(pair_l[long:], up_l),
    ]
    hidden, gate_term, up_term = [], [], []
    for some_gate, some_up in zip(gates, ups):
        some_gate = some_gate.reshape(4, long, units)
        table = some_gate[:, tok : tok + 4].astype(f32) + some_gate[:, tok + 4 : tok + 8].astype(f32)
        signs = some_gate[:, tok + 8, :tok].astype(f32)[:, :, None]
        gate_factor = table[:, 0:1] + signs * table[:, 1:2]
        up_factor = table[:, 2:3] + signs * table[:, 3:4]
        gate = some_gate[:, :tok].astype(f32) * gate_factor
        up = some_up.reshape(4, tok, units).astype(f32) * up_factor
        sig = jax.nn.sigmoid(gate)
        act = gate * sig
        terms = lax.optimization_barrier(
            (
                (act * up).astype(bf16),
                (up * sig * (1.0 + gate * (1.0 - sig)) * gate_factor).astype(bf16),
                (act * up_factor).astype(bf16),
            )
        )
        hidden.append(terms[0])
        gate_term.append(terms[1])
        up_term.append(terms[2])

    down_acc, out_terms = 0.0, 0.0
    for number, part, scaled in ((0, cot_a, scaled_a), (1, cot_b, scaled_b)):
        hid = flat(*[block[:, number * half : (number + 1) * half] for block in hidden])
        down_acc = down_acc + contract_rows(hid, scaled)
        down = jnp.dot(hid, w_down, preferred_element_type=f32).reshape(members, half, width)
        out_terms = out_terms + (part.reshape(members, half, width).astype(f32) * down).sum(axis=1)

    def back_products(number, spread):
        rows = slice(number * half, (number + 1) * half)
        wide = [block.astype(f32) for block in spread]
        pg = flat(*[(a * b[:, rows].astype(f32)).astype(bf16) for a, b in zip(wide, gate_term)])
        pu = flat(*[(a * b[:, rows].astype(f32)).astype(bf16) for a, b in zip(wide, up_term)])
        grad_in = contract_cols(pg, w_gate) + contract_cols(pu, w_up)
        grad_in = grad_in.reshape(members, 2, 2, 2 * sub, width)
        return pg, pu, grad_in, (tok_all[number].astype(f32) * grad_in).sum(axis=(1, 2, 3))

    a_far = jnp.concatenate([a_fr, a_fl])
    a_far, down_grad, out_terms = lax.optimization_barrier((a_far, down_acc.astype(bf16), out_terms))
    pg_a, pu_a, grad_in_a, in_a = back_products(0, [spread_a, a_r, a_far, a_l])
    core_a = add(grad_in_a[:, :, 0], shift(grad_in_a[:, :, 1].astype(bf16), "tc", 1))
    back_1 = shift(core_a[:, 1].astype(bf16), "ty", -1)
    gate_acc, up_acc = contract_rows(in_rows[0], pg_a), contract_rows(in_rows[0], pu_a)

    b_far, gate_acc, up_acc, core_a, in_a = lax.optimization_barrier(
        (jnp.concatenate([b_fr, b_fl]), gate_acc, up_acc, core_a, in_a)
    )
    pg_b, pu_b, grad_in_b, in_b = back_products(1, [spread_b, b_r, b_far, b_l])
    sums = jnp.stack([in_a + in_b, out_terms]).astype(bf16)
    core_b, got = exchange("tc", 1, grad_in_b[:, :, 1].astype(bf16), sums)
    pg_b, pu_b = lax.optimization_barrier((pg_b, pu_b, core_b))[:2]
    gate_acc, up_acc = gate_acc + contract_rows(in_rows[1], pg_b), up_acc + contract_rows(in_rows[1], pu_b)
    sums = add(sums, got).astype(bf16)
    core_b = add(grad_in_b[:, :, 0], core_b).astype(bf16)
    back_2, got = exchange("ty", 2, core_b[:, 0], sums)
    back_3 = shift(core_b[:, 1], "ty", 1)
    sums = add(sums, got).astype(bf16)
    total = add(core_a[:, 0], back_1, back_2, back_3)
    inner, got = exchange("th", 1, total[:, sub:].astype(bf16), sums)
    sums = add(sums, got).astype(bf16)
    inner = (add(total[:, :sub], inner) * in_rel[:, None, :]).astype(bf16).reshape(4, 4, sub, width)
    inner = back_order(back_order(inner, 0, x), 1, z).reshape(members * sub, width)
    x_grad = lax.all_to_all(inner, ("mx", "mz"), 0, 1, tiled=True)
    in_sum, out_sum = add(sums, shift(sums, "ty", 1))
    grad_hidden = jnp.concatenate([own_a, own_b])

    def absolute_table(table):
        table = table.reshape(4, 4, width)
        return back_order(back_order(table, 0, x), 1, z).reshape(members, width)

    pg_f, pu_f = pg_own.astype(f32), pu_own.astype(f32)
    gate = pg_f * (gate_scale + sign * gate_flip)
    up = pu_f * (up_scale + sign * up_flip)
    sig = jax.nn.sigmoid(gate)
    gate_rows = grad_hidden * up * sig * (1.0 + gate * (1.0 - sig)) * pg_f
    up_rows = grad_hidden * gate * sig * pu_f
    return (
        x_grad,
        gate_acc.astype(bf16),
        up_acc.astype(bf16),
        down_grad,
        absolute_table(in_sum),
        absolute_table(out_sum),
        jnp.sum(gate_rows, axis=0, keepdims=True),
        jnp.sum(sign * gate_rows, axis=0, keepdims=True),
        jnp.sum(up_rows, axis=0, keepdims=True),
        jnp.sum(sign * up_rows, axis=0, keepdims=True),
    )


def solution(mesh):
    fine = Mesh(mesh.devices.reshape(tuple(SIZES[axis] for axis in AXES)), AXES)
    member, tensor = ("mx", "mz"), ("ty", "th", "tc")
    both = P(member, tensor)
    return jax.shard_map(
        local,
        mesh=fine,
        in_specs=(
            P(member, None),
            P(member, None),
            P(member),
            P(None, member),
            P(None, member),
            both,
            both,
            both,
            both,
            both,
            both,
            both,
            both,
            P(tensor, member),
        ),
        out_specs=(
            P(member + tensor, None),
            both,
            both,
            P(tensor, member),
            P(None, member),
            P(None, member),
            both,
            both,
            both,
            both,
        ),
        check_vma=False,
    )
```

```python
import jax
import jax.numpy as jnp
from jax import lax
from jax.sharding import Mesh, PartitionSpec as P

AXES = ("mx", "mz", "ty", "th", "tc")
SIZES = {"mx": 4, "mz": 4, "ty": 4, "th": 2, "tc": 2}


def shift(value, axis, step):
    size = SIZES[axis]
    return lax.ppermute(value, axis, [(i, (i + step) % size) for i in range(size)])


def entry(value, index, size=4, dim=0):
    return lax.dynamic_index_in_dim(value, lax.rem(index + size, size), dim, keepdims=False)


def hold(value, *others):
    return lax.optimization_barrier((value, *others))[0]


def contract_rows(left, right):
    return lax.dot_general(left, right, (((0,), (0,)), ((), ())), preferred_element_type=jnp.float32)


def contract_cols(left, right):
    return lax.dot_general(left, right, (((1,), (1,)), ((), ())), preferred_element_type=jnp.float32)


def add(*terms):
    total = terms[0].astype(jnp.float32)
    for term in terms[1:]:
        total = total + term.astype(jnp.float32)
    return total


def exchange(axis, step, *blocks):
    got = shift(jnp.concatenate([block.reshape(-1, block.shape[-1]) for block in blocks]), axis, step)
    out, start = [], 0
    for block in blocks:
        rows = block.size // block.shape[-1]
        out.append(got[start : start + rows].reshape(block.shape))
        start += rows
    return out


def local(
    tokens,
    out_grad,
    flip_bits,
    in_scale,
    out_scale,
    gate_scale,
    gate_flip,
    up_scale,
    up_flip,
    proj_gate,
    proj_up,
    w_gate,
    w_up,
    w_down,
):
    x, z, y, _, c = (lax.axis_index(axis) for axis in AXES)
    tok = tokens.shape[0]
    members, width = in_scale.shape
    units = proj_gate.shape[1]
    half, sub = tok // 2, tok // 16
    f32, bf16 = jnp.float32, jnp.bfloat16

    def to_members(rows):
        blocks = jnp.transpose(rows.reshape(-1, members, width), (1, 0, 2))
        return lax.all_to_all(blocks, ("mx", "mz"), 0, 0, tiled=True)

    rows = [
        lax.dynamic_slice_in_dim(out_grad, c * half, half, 0),
        lax.dynamic_slice_in_dim(tokens, (2 * y + c) * 2 * sub, 2 * sub, 0),
    ]
    own_rows = to_members(jnp.concatenate(rows))
    cot_own, tok_own = own_rows[:, :half], own_rows[:, half:]

    sign = (2 * flip_bits - 1).astype(f32)
    tables = jnp.concatenate([gate_scale, gate_flip, up_scale, up_flip])
    high = lax.reduce_precision(tables, 8, 7)
    piece = jnp.concatenate(
        [
            proj_gate,
            proj_up,
            high.astype(bf16),
            (tables - high).astype(bf16),
            jnp.pad(sign[None, :], ((0, 7), (0, units - tok))).astype(bf16),
        ]
    )
    piece_z = lax.all_gather(hold(piece, cot_own), "mz")

    cot_other = shift(cot_own, "tc", 1)
    tok_own = hold(tok_own, cot_other)
    cot = jnp.concatenate(
        [jnp.where(c == 0, cot_own, cot_other), jnp.where(c == 0, cot_other, cot_own)], axis=1
    )
    grad_z = (cot.astype(f32) * out_scale[:, None, :]).astype(bf16)

    columns = grad_z.reshape(4, 2, 2 * tok, width)

    def partial_sum(step, part):
        return contract_cols(entry(columns, x - step)[part], w_down).astype(bf16)

    parts = lax.optimization_barrier(
        tuple(partial_sum(*part) for part in ((2, 0), (2, 1), (1, 1), (3, 0), (1, 0), (3, 1), (0, 0), (0, 1)))
    )
    near_a, near_b, plain_a, plain_b = lax.optimization_barrier(
        (shift(parts[0], "mx", -1), shift(parts[1], "mx", 1), shift(parts[2], "mx", -1), shift(parts[3], "mx", 1))
    )
    sum_a, sum_b = lax.optimization_barrier(
        (add(parts[4], near_a).astype(bf16), add(parts[5], near_b).astype(bf16))
    )
    sum_a, sum_b = lax.optimization_barrier((shift(sum_a, "mx", -1), shift(sum_b, "mx", 1)))
    piece = lax.all_gather(hold(piece_z, sum_a, sum_b), "mx").reshape(members, 2 * tok + 16, units)
    line = jnp.concatenate([add(parts[6], sum_a, plain_b), add(parts[7], plain_a, sum_b)])
    line = line.astype(bf16).reshape(4, tok, units)
    sent = lax.optimization_barrier(tuple(entry(line, z - k) for k in range(4)))
    got = lax.optimization_barrier(tuple(shift(sent[k], "mz", -k) for k in (1, 2, 3)))
    grad_hidden = add(sent[0], *got)
    own = grad_hidden.astype(bf16)
    got = lax.optimization_barrier(tuple(shift(own, "mz", k) for k in (1, 2, 3)))
    line = jnp.zeros((4, tok, units), bf16)
    for k in range(4):
        line = lax.dynamic_update_index_in_dim(line, got[k - 1] if k else own, lax.rem(z + 4 - k, 4), 0)
    right, left = lax.optimization_barrier((shift(line, "mx", 1), shift(line, "mx", -1)))
    far = jnp.concatenate(lax.optimization_barrier((shift(right[:2], "mx", 1), shift(left[2:], "mx", -1))))

    tok_all = jnp.zeros((4, members, 2 * sub, width), bf16)
    for j in range(4):
        got = tok_own if j == 0 else shift(hold(tok_own, near_a), "ty", j)
        tok_all = lax.dynamic_update_index_in_dim(tok_all, got, lax.rem(y + 4 - j, 4), 0)
    tok_other = shift(tok_all, "tc", 1)
    tok_all = jnp.stack(
        [jnp.where(c == 0, tok_all, tok_other), jnp.where(c == 0, tok_other, tok_all)], axis=1
    )
    tok_all = jnp.transpose(tok_all, (2, 0, 1, 3, 4)).reshape(members, tok, width)
    in_rows = (tok_all.astype(f32) * in_scale[:, None, :]).astype(bf16).reshape(-1, width)

    table = piece[:, 2 * tok : 2 * tok + 4].astype(f32) + piece[:, 2 * tok + 4 : 2 * tok + 8].astype(f32)
    signs = piece[:, 2 * tok + 8, :tok].astype(f32)[:, :, None]
    gate_factor = table[:, 0:1] + signs * table[:, 1:2]
    up_factor = table[:, 2:3] + signs * table[:, 3:4]
    gate = piece[:, :tok].astype(f32) * gate_factor
    up = piece[:, tok : 2 * tok].astype(f32) * up_factor
    sig = jax.nn.sigmoid(gate)
    act = gate * sig
    hidden, gate_term, up_term = lax.optimization_barrier(
        (
            (act * up).astype(bf16),
            (up * sig * (1.0 + gate * (1.0 - sig)) * gate_factor).astype(bf16),
            (act * up_factor).astype(bf16),
        )
    )
    hidden = hidden.reshape(-1, units)
    rows = grad_z.reshape(-1, width)
    down_grad = contract_rows(hidden, rows).astype(bf16)
    down = jnp.dot(hidden, w_down, preferred_element_type=f32).reshape(members, tok, width)
    out_terms = (cot.astype(f32) * down).sum(axis=1)
    far, down_grad, out_terms = lax.optimization_barrier((far, down_grad, out_terms))

    gate_term, up_term = (term.reshape(4, 4, tok, units) for term in (gate_term, up_term))
    pg, pu = jnp.zeros((4, 4, tok, units), bf16), jnp.zeros((4, 4, tok, units), bf16)
    for step, block in ((0, line), (1, right), (3, left), (2, far)):
        place = lax.rem(x + 4 - step, 4)
        block = block.astype(f32)
        one = (block * entry(gate_term, place).astype(f32)).astype(bf16)
        two = (block * entry(up_term, place).astype(f32)).astype(bf16)
        pg = lax.dynamic_update_index_in_dim(pg, one, place, 0)
        pu = lax.dynamic_update_index_in_dim(pu, two, place, 0)
    pg, pu = pg.reshape(-1, units), pu.reshape(-1, units)
    grad_in = contract_cols(pg, w_gate) + contract_cols(pu, w_up)
    grad_in = grad_in.reshape(members, tok, width)
    in_terms = (tok_all.astype(f32) * grad_in).sum(axis=1)
    sums = jnp.stack([in_terms, out_terms]).astype(bf16)

    by_core = grad_in.reshape(members, 8, 2, sub, width)
    core, got = exchange("tc", 1, entry(by_core, 1 - c, 2, 2).astype(bf16), sums)
    pg, pu = lax.optimization_barrier((pg, pu, core))[:2]
    gate_grad = contract_rows(in_rows, pg).astype(bf16)
    up_grad = contract_rows(in_rows, pu).astype(bf16)
    sums = add(sums, got).astype(bf16)
    core = add(entry(by_core, c, 2, 2), core).reshape(members, 4, 2, sub, width)
    sent = [entry(core, y - j, 4, 1).astype(bf16) for j in (1, 2, 3)]
    back_2, got = exchange("ty", 2, sent[1], sums)
    back_1, back_3 = shift(sent[0], "ty", -1), shift(sent[2], "ty", 1)
    sums = add(sums, got).astype(bf16)
    inner = add(entry(core, y, 4, 1), back_1, back_2, back_3) * in_scale[:, None, None, :]
    inner = inner.astype(bf16).reshape(2 * members, sub, width)
    inner = lax.all_to_all(inner, ("mx", "mz", "th"), 0, 0, tiled=True)
    inner = inner.reshape(members, 2, sub, width)
    x_grad = add(inner[:, 0], inner[:, 1]).astype(bf16)
    x_grad = jnp.transpose(x_grad, (1, 0, 2)).reshape(sub, members * width)
    sums = add(sums, shift(sums, "th", 1)).astype(bf16)
    in_sum, out_sum = add(sums, shift(sums, "ty", 1))

    sign = sign[:, None]
    pg_f, pu_f = proj_gate.astype(f32), proj_up.astype(f32)
    gate = pg_f * (gate_scale + sign * gate_flip)
    up = pu_f * (up_scale + sign * up_flip)
    sig = jax.nn.sigmoid(gate)
    gate_rows = grad_hidden * up * sig * (1.0 + gate * (1.0 - sig)) * pg_f
    up_rows = grad_hidden * gate * sig * pu_f
    return (
        x_grad,
        gate_grad,
        up_grad,
        down_grad,
        in_sum,
        out_sum,
        jnp.sum(gate_rows, axis=0, keepdims=True),
        jnp.sum(sign * gate_rows, axis=0, keepdims=True),
        jnp.sum(up_rows, axis=0, keepdims=True),
        jnp.sum(sign * up_rows, axis=0, keepdims=True),
    )


def solution(mesh):
    fine = Mesh(mesh.devices.reshape(tuple(SIZES[axis] for axis in AXES)), AXES)
    member, tensor = ("mx", "mz"), ("ty", "th", "tc")
    both = P(member, tensor)
    return jax.shard_map(
        local,
        mesh=fine,
        in_specs=(
            P(member, None),
            P(member, None),
            P(member),
            P(None, member),
            P(None, member),
            both,
            both,
            both,
            both,
            both,
            both,
            both,
            both,
            P(tensor, member),
        ),
        out_specs=(
            P(member + tensor, None),
            both,
            both,
            P(tensor, member),
            P(None, member),
            P(None, member),
            both,
            both,
            both,
            both,
        ),
        check_vma=False,
    )
```

```python
import jax
import jax.numpy as jnp
from jax import lax
from jax.sharding import Mesh, PartitionSpec as P

AXES = ("mx", "mz", "ty", "th", "tc")
SIZES = {"mx": 4, "mz": 4, "ty": 4, "th": 2, "tc": 2}


def shift(value, axis, step):
    size = SIZES[axis]
    return lax.ppermute(value, axis, [(i, (i + step) % size) for i in range(size)])


def entry(value, index, size=4, dim=0):
    return lax.dynamic_index_in_dim(value, lax.rem(index + size, size), dim, keepdims=False)


def hold(value, *others):
    return lax.optimization_barrier((value, *others))[0]


def contract_rows(left, right):
    return lax.dot_general(left, right, (((0,), (0,)), ((), ())), preferred_element_type=jnp.float32)


def contract_cols(left, right):
    return lax.dot_general(left, right, (((1,), (1,)), ((), ())), preferred_element_type=jnp.float32)


def add(*terms):
    total = terms[0].astype(jnp.float32)
    for term in terms[1:]:
        total = total + term.astype(jnp.float32)
    return total


def exchange(axis, step, *blocks):
    got = shift(jnp.concatenate([block.reshape(-1, block.shape[-1]) for block in blocks]), axis, step)
    out, start = [], 0
    for block in blocks:
        rows = block.size // block.shape[-1]
        out.append(got[start : start + rows].reshape(block.shape))
        start += rows
    return out


def local(
    tokens,
    out_grad,
    flip_bits,
    in_scale,
    out_scale,
    gate_scale,
    gate_flip,
    up_scale,
    up_flip,
    proj_gate,
    proj_up,
    w_gate,
    w_up,
    w_down,
):
    x, z, y, _, c = (lax.axis_index(axis) for axis in AXES)
    tok = tokens.shape[0]
    members, width = in_scale.shape
    units = proj_gate.shape[1]
    half, sub = tok // 2, tok // 16
    f32, bf16 = jnp.float32, jnp.bfloat16

    def to_members(rows):
        blocks = jnp.transpose(rows.reshape(-1, members, width), (1, 0, 2))
        return lax.all_to_all(blocks, ("mx", "mz"), 0, 0, tiled=True)

    sign = (2 * flip_bits - 1).astype(f32)
    tables = jnp.concatenate([gate_scale, gate_flip, up_scale, up_flip])
    high = lax.reduce_precision(tables, 8, 7)
    piece = jnp.concatenate(
        [
            proj_gate,
            proj_up,
            high.astype(bf16),
            (tables - high).astype(bf16),
            jnp.pad(sign[None, :], ((0, 7), (0, units - tok))).astype(bf16),
        ]
    )
    own_x = lax.all_gather(piece, "mx")

    rows = [
        lax.dynamic_slice_in_dim(out_grad, c * half, half, 0),
        lax.dynamic_slice_in_dim(tokens, (2 * y + c) * 2 * sub, 2 * sub, 0),
    ]
    own_rows = to_members(hold(jnp.concatenate(rows), piece))
    cot_own, tok_own = own_rows[:, :half], own_rows[:, half:]

    piece_z = lax.all_gather(hold(piece, cot_own), "mz")

    cot_other = shift(cot_own, "tc", 1)
    tok_own = hold(tok_own, cot_other)
    cot = jnp.concatenate(
        [jnp.where(c == 0, cot_own, cot_other), jnp.where(c == 0, cot_other, cot_own)], axis=1
    )
    grad_z = (cot.astype(f32) * out_scale[:, None, :]).astype(bf16)

    columns = grad_z.reshape(4, 2, 2 * tok, width)

    def partial_sum(step, part):
        return contract_cols(entry(columns, x - step)[part], w_down).astype(bf16)

    parts = lax.optimization_barrier(
        tuple(partial_sum(*part) for part in ((2, 0), (2, 1), (1, 1), (3, 0), (1, 0), (3, 1), (0, 0), (0, 1)))
    )
    near_a, near_b, plain_a, plain_b, own_x = lax.optimization_barrier(
        (
            shift(parts[0], "mx", -1),
            shift(parts[1], "mx", 1),
            shift(parts[2], "mx", -1),
            shift(parts[3], "mx", 1),
            own_x,
        )
    )
    sum_a, sum_b = lax.optimization_barrier(
        (add(parts[4], near_a).astype(bf16), add(parts[5], near_b).astype(bf16))
    )
    sum_a, sum_b = lax.optimization_barrier((shift(sum_a, "mx", -1), shift(sum_b, "mx", 1)))
    piece_z = hold(piece_z, sum_a, sum_b)
    rest_x = lax.all_gather(jnp.stack([entry(piece_z, z + k) for k in (1, 2, 3)]), "mx")
    line = jnp.concatenate([add(parts[6], sum_a, plain_b), add(parts[7], plain_a, sum_b)])
    line = line.astype(bf16).reshape(4, tok, units)
    sent = lax.optimization_barrier(tuple(entry(line, z - k) for k in range(4)))
    got = lax.optimization_barrier(tuple(shift(sent[k], "mz", -k) for k in (1, 2, 3)))
    grad_hidden = add(sent[0], *got)
    own = grad_hidden.astype(bf16)
    got = lax.optimization_barrier(tuple(shift(own, "mz", k) for k in (1, 2, 3)))
    line = jnp.zeros((4, tok, units), bf16)
    for k in range(4):
        line = lax.dynamic_update_index_in_dim(line, got[k - 1] if k else own, lax.rem(z + 4 - k, 4), 0)
    right, left = lax.optimization_barrier((shift(line, "mx", 1), shift(line, "mx", -1)))

    tok_all = jnp.zeros((4, members, 2 * sub, width), bf16)
    for j in range(4):
        got = tok_own if j == 0 else shift(hold(tok_own, near_a), "ty", j)
        tok_all = lax.dynamic_update_index_in_dim(tok_all, got, lax.rem(y + 4 - j, 4), 0)
    tok_other = shift(tok_all, "tc", 1)
    tok_all = jnp.stack(
        [jnp.where(c == 0, tok_all, tok_other), jnp.where(c == 0, tok_other, tok_all)], axis=1
    )
    tok_all = jnp.transpose(tok_all, (2, 0, 1, 3, 4)).reshape(members, tok, width)
    in_rows = (tok_all.astype(f32) * in_scale[:, None, :]).astype(bf16).reshape(-1, width)

    piece = jnp.zeros((4, 4, 2 * tok + 16, units), bf16)
    for k in range(4):
        got = rest_x[:, k - 1] if k else own_x
        piece = lax.dynamic_update_index_in_dim(piece, got, lax.rem(z + k, 4), 1)
    piece = piece.reshape(members, 2 * tok + 16, units)
    table = piece[:, 2 * tok : 2 * tok + 4].astype(f32) + piece[:, 2 * tok + 4 : 2 * tok + 8].astype(f32)
    signs = piece[:, 2 * tok + 8, :tok].astype(f32)[:, :, None]
    gate_factor = table[:, 0:1] + signs * table[:, 1:2]
    up_factor = table[:, 2:3] + signs * table[:, 3:4]
    gate = piece[:, :tok].astype(f32) * gate_factor
    up = piece[:, tok : 2 * tok].astype(f32) * up_factor
    sig = jax.nn.sigmoid(gate)
    act = gate * sig
    hidden, gate_term, up_term = lax.optimization_barrier(
        (
            (act * up).astype(bf16),
            (up * sig * (1.0 + gate * (1.0 - sig)) * gate_factor).astype(bf16),
            (act * up_factor).astype(bf16),
        )
    )
    far = (hold(right[:2], gate_term), hold(left[2:], gate_term))
    far = jnp.concatenate(lax.optimization_barrier((shift(far[0], "mx", 1), shift(far[1], "mx", -1))))
    hidden = hidden.reshape(-1, units)
    rows = grad_z.reshape(-1, width)
    down_grad = contract_rows(hidden, rows).astype(bf16)
    down = jnp.dot(hidden, w_down, preferred_element_type=f32).reshape(members, tok, width)
    out_terms = (cot.astype(f32) * down).sum(axis=1)
    far, down_grad, out_terms = lax.optimization_barrier((far, down_grad, out_terms))

    gate_term, up_term = (term.reshape(4, 4, tok, units) for term in (gate_term, up_term))
    pg, pu = jnp.zeros((4, 4, tok, units), bf16), jnp.zeros((4, 4, tok, units), bf16)
    for step, block in ((0, line), (1, right), (3, left), (2, far)):
        place = lax.rem(x + 4 - step, 4)
        block = block.astype(f32)
        one = (block * entry(gate_term, place).astype(f32)).astype(bf16)
        two = (block * entry(up_term, place).astype(f32)).astype(bf16)
        pg = lax.dynamic_update_index_in_dim(pg, one, place, 0)
        pu = lax.dynamic_update_index_in_dim(pu, two, place, 0)
    pg, pu = pg.reshape(-1, units), pu.reshape(-1, units)
    grad_in = contract_cols(pg, w_gate) + contract_cols(pu, w_up)
    grad_in = grad_in.reshape(members, tok, width)
    in_terms = (tok_all.astype(f32) * grad_in).sum(axis=1)
    sums = jnp.stack([in_terms, out_terms]).astype(bf16)

    by_core = grad_in.reshape(members, 8, 2, sub, width)
    core, got = exchange("tc", 1, entry(by_core, 1 - c, 2, 2).astype(bf16), sums)
    pg, pu = lax.optimization_barrier((pg, pu, core))[:2]
    gate_grad = contract_rows(in_rows, pg).astype(bf16)
    up_grad = contract_rows(in_rows, pu).astype(bf16)
    sums = add(sums, got).astype(bf16)
    core = add(entry(by_core, c, 2, 2), core).reshape(members, 4, 2, sub, width)
    sent = [entry(core, y - j, 4, 1).astype(bf16) for j in (1, 2, 3)]
    back_2, got, back_1, back_3 = lax.optimization_barrier(
        (*exchange("ty", 2, sent[1], sums), shift(sent[0], "ty", -1), shift(sent[2], "ty", 1))
    )
    sums = add(sums, got).astype(bf16)
    inner = add(entry(core, y, 4, 1), back_1, back_2, back_3) * in_scale[:, None, None, :]
    inner = inner.astype(bf16).reshape(2 * members, sub, width)
    inner = lax.all_to_all(inner, ("mx", "mz", "th"), 0, 0, tiled=True)
    inner = inner.reshape(members, 2, sub, width)
    x_grad = add(inner[:, 0], inner[:, 1]).astype(bf16)
    x_grad = jnp.transpose(x_grad, (1, 0, 2)).reshape(sub, members * width)
    sums = add(sums, shift(sums, "th", 1)).astype(bf16)
    in_sum, out_sum = add(sums, shift(sums, "ty", 1))

    sign = sign[:, None]
    pg_f, pu_f = proj_gate.astype(f32), proj_up.astype(f32)
    gate = pg_f * (gate_scale + sign * gate_flip)
    up = pu_f * (up_scale + sign * up_flip)
    sig = jax.nn.sigmoid(gate)
    gate_rows = grad_hidden * up * sig * (1.0 + gate * (1.0 - sig)) * pg_f
    up_rows = grad_hidden * gate * sig * pu_f
    return (
        x_grad,
        gate_grad,
        up_grad,
        down_grad,
        in_sum,
        out_sum,
        jnp.sum(gate_rows, axis=0, keepdims=True),
        jnp.sum(sign * gate_rows, axis=0, keepdims=True),
        jnp.sum(up_rows, axis=0, keepdims=True),
        jnp.sum(sign * up_rows, axis=0, keepdims=True),
    )


def solution(mesh):
    fine = Mesh(mesh.devices.reshape(tuple(SIZES[axis] for axis in AXES)), AXES)
    member, tensor = ("mx", "mz"), ("ty", "th", "tc")
    both = P(member, tensor)
    return jax.shard_map(
        local,
        mesh=fine,
        in_specs=(
            P(member, None),
            P(member, None),
            P(member),
            P(None, member),
            P(None, member),
            both,
            both,
            both,
            both,
            both,
            both,
            both,
            both,
            P(tensor, member),
        ),
        out_specs=(
            P(member + tensor, None),
            both,
            both,
            P(tensor, member),
            P(None, member),
            P(None, member),
            both,
            both,
            both,
            both,
        ),
        check_vma=False,
    )
```
